32 devices in a mesh: dp: 4 (over z), ctx: 8 (over y, x, core).
Axes of the slice: x: 2, y: 2, z: 4, core: 2. Of those that a mesh axis runs over, the one named last changes fastest.
Arguments:
- queries: bfloat16 [4, 1024, 6144], P('dp', 'ctx'), may hold values from -6 to 6
- kv_proj: bfloat16 [4, 3072, 1024], P('dp', 'ctx'), may hold values from -6 to 6
- hidden: bfloat16 [4, 3072, 12288], P('dp', 'ctx'), may hold values from -0.119628906 to 0.119628906
- grad_out: bfloat16 [4, 1024, 6144], P('dp', 'ctx'), may hold values from -6 to 6
- doc_lengths: int32 [4, 256], P('dp'), may hold values from 1 to 8192, 262144 in all within a row
- slab_offsets: int32 [4], P('dp'), may hold values from 0 to 261120
Outputs:
- attended: bfloat16 [4, 1024, 6144], P('dp', 'ctx')
- grad_queries: bfloat16 [4, 1024, 6144], P('dp', 'ctx')
- grad_kv: bfloat16 [4, 3072, 1024], P('dp', 'ctx')
- grad_weight: float32 [12288, 1024], P('ctx', 'dp')
The draws below stay inside these ranges and needn't reach their ends.
All inputs are finite; a program needn't handle non-finite values.
Results may differ from the reference program's by a relative error of at most 0.025.
Values may be sent and summed in bfloat16 or wider, within the bound.
A program may use at most 192 MiB of HBM per device.

```python
import math
import jax
import jax.numpy as jnp
import numpy as np
from jax import lax

D = 12288
HEAD_FEATURES = 128
QUERY_HEADS = 48
KEY_VALUE_HEADS = 4
WINDOW = 2048
SEQ_LEN = 262144
NDOCS = 256
MOST = 8192
PACKED_SEQUENCES = 4
SLAB = 1024
KEY_POSITIONS = 3072


def paired_draw(key):
    base = jax.random.fold_in(key, 811)
    key_query, key_pair = jax.random.split(base, 2)
    query_shape = (PACKED_SEQUENCES, SLAB, QUERY_HEADS * HEAD_FEATURES)
    key_value_shape = (PACKED_SEQUENCES, KEY_POSITIONS, KEY_VALUE_HEADS * 2 * HEAD_FEATURES)
    query_vals = jnp.clip(jax.random.normal(key_query, query_shape, jnp.float32), -6.0, 6.0)
    key_value_entries = jnp.clip(jax.random.normal(key_pair, key_value_shape, jnp.float32), -6.0, 6.0)
    return (query_vals, key_value_entries)


def draw_queries(key, part):
    return paired_draw(key)[0].astype(jnp.bfloat16)


def draw_kv_proj(key, part):
    return paired_draw(key)[1].astype(jnp.bfloat16)


def place_ends(values, own_key, least, largest):
    longest = values.shape.index(max(values.shape))
    spots = []
    for shift in (0, 1):
        where = [jax.random.randint(jax.random.fold_in(own_key, axis), (), 0, length) for axis, length in enumerate(values.shape)]
        where[longest] = (where[longest] + shift) % values.shape[longest]
        spots.append(tuple(where))
    return values.at[spots[0]].set(least).at[spots[1]].set(largest)


def spiked(entries, own_key, source, target, parts, factor):
    def block_of(position):
        return (jnp.arange(entries.shape[position]) // (entries.shape[position] // parts)).reshape((-1,) + (1,) * (entries.ndim - 1 - position))

    first = jax.random.permutation(own_key, parts)[block_of(target)]
    other_side = (block_of(target) + parts // 2) % parts
    return jnp.where((block_of(source) == first) | (block_of(source) == other_side), factor * entries, entries)


def shard_levels(key, dims, shards, smallest, largest):
    def one(position, parts):
        steps = jax.random.uniform(jax.random.fold_in(jax.random.fold_in(key, 6), position), (parts,), jnp.float32, smallest / len(shards), largest / len(shards))
        return jnp.repeat(jnp.exp(steps), dims[position] // parts).reshape((-1,) + (1,) * (len(dims) - position - 1))

    level = one(*shards[0])
    for cut in shards[1:]:
        level = level * one(*cut)
    return level


def split_up(number_of, total, most, lean):
    portions = [(1 << 20) // math.isqrt(standing ** lean) + 1 for standing in range(2, number_of + 1)]
    surplus, holding = total - most - (number_of - 1), [1] * (number_of - 1)
    while surplus > 0:
        candidates = [i for i in range(number_of - 1) if holding[i] < most]
        mass, left = sum([portions[i] for i in candidates]), surplus
        for i in candidates:
            more = min(most - holding[i], max(1, left * portions[i] // mass), surplus)
            holding[i] = holding[i] + more
            surplus = surplus - more
    return np.array([most] + holding)


def uneven(key, number_of, total, reach, skew):
    if number_of == 2:
        one = jax.random.randint(key, (), max(1, total - reach), min(reach, total - 1) + 1)
        return jnp.stack([one, total - one])
    sizes = jnp.asarray(split_up(number_of, total, reach, skew), jnp.int32)
    couples = (number_of - 1) // 2
    giver, sink = sizes[1:1 + 2 * couples:2], sizes[2:2 + 2 * couples:2]
    slack = jnp.minimum(giver - 1, reach - sink)
    shifted = jax.random.randint(jax.random.fold_in(key, 1), (couples,), 0, 1 << 20) % (slack + 1)
    sizes = sizes.at[1:1 + 2 * couples:2].set(giver - shifted).at[2:2 + 2 * couples:2].set(sink + shifted)
    return sizes[jax.random.permutation(jax.random.fold_in(key, 2), number_of)]


def bell_draw(key, dims, spread, most, pieces=(), kind=jnp.bfloat16):
    drawn = jax.random.normal(key, dims, jnp.float32) * spread
    if len(pieces) > 0:
        drawn = shard_levels(key, dims, pieces, -0.22, 0.18) * drawn
    return jnp.clip(drawn, min=-most, max=most).astype(kind)


def gaussian_with(stream_key, shape, deviation, bound, cuts, heavy, held_as=jnp.bfloat16):
    drawn = deviation * jax.random.normal(stream_key, shape, jnp.float32)
    if cuts:
        drawn = drawn * shard_levels(stream_key, shape, cuts, -0.22, 0.18)
    return jnp.clip(spiked(drawn, jax.random.fold_in(stream_key, 3), *heavy), -bound, bound).astype(held_as)


def setup_inputs(seed: int = 0) -> dict:
    arg_keys = jax.random.split(jax.random.key(seed), 7)
    return {
        "queries": draw_queries(jax.random.fold_in(arg_keys[6], 71), 0),
        "kv_proj": draw_kv_proj(jax.random.fold_in(arg_keys[6], 71), 0),
        "hidden": gaussian_with(arg_keys[2], (PACKED_SEQUENCES, KEY_POSITIONS, D), 0.02, 0.119628906, ((0, 4), (1, 8)), (1, 2, 8, 2.0)),
        "grad_out": bell_draw(arg_keys[3], (PACKED_SEQUENCES, SLAB, QUERY_HEADS * HEAD_FEATURES), 1.0, 6.0, ((0, 4), (1, 8))),
        "doc_lengths": jax.vmap(lambda own: uneven(own, NDOCS, SEQ_LEN, MOST, 2))(jax.random.split(arg_keys[4], PACKED_SEQUENCES)).reshape((PACKED_SEQUENCES, NDOCS)).astype(jnp.int32),
        "slab_offsets": place_ends(jax.random.randint(arg_keys[5], (PACKED_SEQUENCES,), 0, SEQ_LEN - SLAB + 1), jax.random.fold_in(arg_keys[5], 1), 0, SEQ_LEN - SLAB).astype(jnp.int32),
    }


def doc_index(positions, bounds):
    return jnp.sum((bounds[None, :] <= positions[:, None]).astype(jnp.int32), axis=1, dtype=jnp.int32)


def band_mask(anchor, row_count, key_span, offset, bounds):
    query_index = anchor + jnp.arange(row_count, dtype=jnp.int32)
    key_index = anchor + jnp.arange(key_span, dtype=jnp.int32)
    query_pos = offset + query_index
    key_pos = offset - WINDOW + key_index
    same_doc = doc_index(query_pos, bounds)[:, None] == doc_index(key_pos, bounds)[None, :]
    after_query = key_index[None, :] > query_index[:, None]
    within = key_index[None, :] <= query_index[:, None] + WINDOW
    return after_query & within & (key_pos >= 0)[None, :] & same_doc


def band_block(query_block, key_block, value_block, upstream_gradient, allowed):
    factor = HEAD_FEATURES ** -0.5
    f32 = jnp.float32
    scores = jnp.einsum("qhgd,khd->hgqk", query_block.astype(f32), key_block.astype(f32)) * factor
    scores = jnp.where(allowed[None, None], scores, -1e30)
    maxima = jnp.max(scores, axis=-1, keepdims=True)
    raised = jnp.exp(scores - maxima)
    weights = raised / jnp.sum(raised, axis=-1, keepdims=True)
    weights_low = weights.astype(jnp.bfloat16)
    attended = jnp.einsum("hgqk,khd->qhgd", weights_low.astype(f32), value_block.astype(f32)).astype(jnp.bfloat16)
    grad_probs = jnp.einsum("qhgd,khd->hgqk", upstream_gradient.astype(f32), value_block.astype(f32))
    deltas = jnp.einsum("qhgd,qhgd->hgq", upstream_gradient.astype(f32), attended.astype(f32))
    grad_scores = (weights * (grad_probs - deltas[..., None]) * factor).astype(jnp.bfloat16)
    grad_query = jnp.einsum("hgqk,khd->qhgd", grad_scores.astype(f32), key_block.astype(f32)).astype(jnp.bfloat16)
    grad_key = jnp.einsum("hgqk,qhgd->khd", grad_scores.astype(f32), query_block.astype(f32))
    grad_value = jnp.einsum("hgqk,qhgd->khd", weights_low.astype(f32), upstream_gradient.astype(f32))
    return attended, grad_query, jnp.stack([grad_key, grad_value], axis=2)


def band_attention(query_all, upstream_all, pair_all, anchor, offset, bounds, block_rows):
    query_total_count = query_all.shape[0]
    key_total_count = pair_all.shape[0]
    head_count = query_all.shape[1]
    key_span = block_rows + WINDOW

    def step(running, block_index):
        first_row = block_index * block_rows
        query_block = lax.dynamic_slice_in_dim(query_all, first_row, block_rows, 0)
        upstream_gradient = lax.dynamic_slice_in_dim(upstream_all, first_row, block_rows, 0)
        pair_block = lax.dynamic_slice_in_dim(pair_all, first_row, key_span, 0)
        allowed = band_mask(anchor + first_row, block_rows, key_span, offset, bounds)
        attended, grad_query, grad_pair = band_block(query_block, pair_block[:, :, 0], pair_block[:, :, 1], upstream_gradient, allowed)
        previous = lax.dynamic_slice_in_dim(running, first_row, key_span, 0)
        running = lax.dynamic_update_slice_in_dim(running, previous + grad_pair, first_row, 0)
        return running, (attended, grad_query)

    initial = jnp.zeros((key_total_count, head_count, 2, HEAD_FEATURES), jnp.float32)
    grads, outputs = lax.scan(step, initial, jnp.arange(query_total_count // block_rows, dtype=jnp.int32))
    attended, grad_query = outputs
    return attended.reshape(query_total_count, -1), grad_query.reshape(query_total_count, -1), grads.reshape(key_total_count, -1)


def reference(queries, kv_proj, hidden, grad_out, doc_lengths, slab_offsets):
    queries_per_group = QUERY_HEADS // KEY_VALUE_HEADS

    def one_sequence(running, inputs):
        query_matrix_rows, key_matrix_rows, hidden_rows, upstream_gradient, lengths, offset = inputs
        bounds = jnp.cumsum(lengths, dtype=jnp.int32)
        query_total_count = query_matrix_rows.shape[0]
        attended, grad_query, grad_keys = band_attention(
            query_matrix_rows.reshape(query_total_count, KEY_VALUE_HEADS, queries_per_group, HEAD_FEATURES),
            upstream_gradient.reshape(query_total_count, KEY_VALUE_HEADS, queries_per_group, HEAD_FEATURES),
            key_matrix_rows.reshape(key_matrix_rows.shape[0], KEY_VALUE_HEADS, 2, HEAD_FEATURES),
            0, offset, bounds, min(512, query_total_count))
        grad_low = grad_keys.astype(jnp.bfloat16)
        running = running + jnp.dot(hidden_rows.T, grad_low, preferred_element_type=jnp.float32)
        return running, (attended, grad_query, grad_low)

    initial = jnp.zeros((hidden.shape[2], kv_proj.shape[2]), jnp.float32)
    grad_weight, outputs = lax.scan(one_sequence, initial, (queries, kv_proj, hidden, grad_out, doc_lengths, slab_offsets))
    attended, grad_queries, grad_kv = outputs
    return (attended, grad_queries, grad_kv, grad_weight)
```

```python
import functools

import jax
import jax.numpy as jnp
from jax import lax
from jax.experimental import pallas as pl
from jax.experimental.pallas import tpu as pltpu
from jax.sharding import PartitionSpec as P

HD = 128
KV_HEADS = 4
WINDOW = 2048
BLK = 256
LOG2E = 1.4426950408889634
FACTOR = HD ** (-0.5)
NT = (((1,), (1,)), ((), ()))
TN = (((0,), (0,)), ((), ()))
NN = (((1,), (0,)), ((), ()))


def dot(a, b, dims=NN):
    return lax.dot_general(a, b, dims, preferred_element_type=jnp.float32)


def attention_kernel(
    heads, lo_ref, low_ref, q_ref, go_ref, kv_ref, out_ref, grads_ref,
    scores, kt, vt, qs, gs, wlow, dlow, mx, tot, acc, delta,
):
    f32, bf16 = jnp.float32, jnp.bfloat16
    qb = pl.program_id(0)
    chunks = kt.shape[0]

    @pl.when(qb == 0)
    def _():
        grads_ref[...] = jnp.zeros_like(grads_ref)

        def prep(c, carry):
            rows = pl.ds(pl.multiple_of(c * BLK, BLK), BLK)
            kt[c] = kv_ref[rows, :HD].astype(f32).T.astype(bf16)
            vt[c] = kv_ref[rows, HD:].astype(f32).T.astype(bf16)
            return carry

        lax.fori_loop(0, chunks, prep, 0)

    for h in range(heads):
        qs[h * BLK : (h + 1) * BLK] = q_ref[:, h * HD : (h + 1) * HD]
        gs[h * BLK : (h + 1) * BLK] = go_ref[:, h * HD : (h + 1) * HD]
    mx[...] = jnp.full(mx.shape, -1e30, f32)
    tot[...] = jnp.zeros(tot.shape, f32)
    acc[...] = jnp.zeros(acc.shape, f32)
    first = lo_ref[qb]
    last = qb + WINDOW // BLK + 1
    low = low_ref[...]
    lane = lax.broadcasted_iota(jnp.int32, (BLK, BLK), 1)
    sub = lax.broadcasted_iota(jnp.int32, (BLK, BLK), 0)

    def score_step(c, carry):
        rows = pl.ds(pl.multiple_of(c * BLK, BLK), BLK)
        key = kv_ref[rows, :HD]
        j = sub + c * BLK
        ok = (j >= low) & (j <= lane + (qb * BLK + WINDOW))
        for h in range(heads):
            cols = slice(h * BLK, (h + 1) * BLK)
            s = dot(key, qs[cols, :], NT)
            s = jnp.where(ok, s, -1e30)
            scores[c - qb, :, cols] = s
            part = jnp.max(s.reshape(BLK // 8, 8, BLK), axis=0)
            mx[:, cols] = jnp.maximum(mx[:, cols], part)
        return carry

    lax.fori_loop(first, last, score_step, 0)
    mx[0:1, :] = jnp.max(mx[...], axis=0, keepdims=True) * (FACTOR * LOG2E)

    def value_step(c, carry):
        for h in range(heads):
            cols = slice(h * BLK, (h + 1) * BLK)
            p = jnp.exp2(scores[c - qb, :, cols] * (FACTOR * LOG2E) - mx[0:1, cols])
            scores[c - qb, :, cols] = p
            tot[:, cols] += jnp.sum(p.reshape(BLK // 8, 8, BLK), axis=0)
            acc[:, cols] += dot(vt[c], p.astype(bf16))
        return carry

    lax.fori_loop(first, last, value_step, 0)
    tot[0:1, :] = 1.0 / jnp.sum(tot[...], axis=0, keepdims=True)
    for h in range(heads):
        cols = slice(h * BLK, (h + 1) * BLK)
        att = (acc[:, cols] * tot[0:1, cols]).T.astype(bf16)
        out_ref[0, :, h * HD : (h + 1) * HD] = att
        prod = att.astype(f32) * gs[cols, :].astype(f32)
        delta[0:1, cols] = jnp.sum(prod.T, axis=0, keepdims=True)
    acc[...] = jnp.zeros(acc.shape, f32)

    def grad_step(c, carry):
        rows = pl.ds(pl.multiple_of(c * BLK, BLK), BLK)
        value = kv_ref[rows, HD:]
        for h in range(heads):
            cols = slice(h * BLK, (h + 1) * BLK)
            w = scores[c - qb, :, cols] * tot[0:1, cols]
            gp = dot(value, gs[cols, :], NT)
            ds = (w * (gp - delta[0:1, cols])).astype(bf16)
            wlow[:, cols] = w.astype(bf16)
            dlow[:, cols] = ds
            acc[:, cols] += dot(kt[c], ds)
        grads_ref[rows, :HD] += dot(dlow[...], qs[...]) * FACTOR
        grads_ref[rows, HD:] += dot(wlow[...], gs[...])
        return carry

    lax.fori_loop(first, last, grad_step, 0)
    for h in range(heads):
        cols = slice(h * BLK, (h + 1) * BLK)
        out_ref[1, :, h * HD : (h + 1) * HD] = (acc[:, cols] * FACTOR).T.astype(bf16)


def attention(first, low, q, go, kv):
    rows, width = q.shape
    keys = kv.shape[0]
    heads = width // HD
    f32, bf16 = jnp.float32, jnp.bfloat16
    wide = heads * BLK
    span = WINDOW // BLK + 1
    chunks = keys // BLK
    blk = pl.BlockSpec((BLK, width), lambda i, s: (i, 0))
    return pl.pallas_call(
        functools.partial(attention_kernel, heads),
        grid_spec=pltpu.PrefetchScalarGridSpec(
            num_scalar_prefetch=1,
            grid=(rows // BLK,),
            in_specs=[
                pl.BlockSpec((1, BLK), lambda i, s: (0, i)),
                blk,
                blk,
                pl.BlockSpec((keys, 2 * HD), lambda i, s: (0, 0)),
            ],
            out_specs=[
                pl.BlockSpec((2, BLK, width), lambda i, s: (0, i, 0)),
                pl.BlockSpec((keys, 2 * HD), lambda i, s: (0, 0)),
            ],
            scratch_shapes=[
                pltpu.VMEM((span, BLK, wide), f32),
                pltpu.VMEM((chunks, HD, BLK), bf16),
                pltpu.VMEM((chunks, HD, BLK), bf16),
                pltpu.VMEM((wide, HD), bf16),
                pltpu.VMEM((wide, HD), bf16),
                pltpu.VMEM((BLK, wide), bf16),
                pltpu.VMEM((BLK, wide), bf16),
                pltpu.VMEM((8, wide), f32),
                pltpu.VMEM((8, wide), f32),
                pltpu.VMEM((HD, wide), f32),
                pltpu.VMEM((8, wide), f32),
            ],
        ),
        out_shape=[
            jax.ShapeDtypeStruct((2, rows, width), bf16),
            jax.ShapeDtypeStruct((keys, 2 * HD), f32),
        ],
        compiler_params=pltpu.CompilerParams(vmem_limit_bytes=48 * 1024 * 1024),
        cost_estimate=pl.CostEstimate(
            flops=20 * rows * (WINDOW + BLK) * width * 4,
            bytes_accessed=12 * rows * width,
            transcendentals=rows * (WINDOW + BLK) * heads,
        ),
        name="attention",
    )(first, low, q, go, kv)


def weight_kernel(count, idx_ref, g_ref, *refs):
    out_ref = refs[count]
    total = None
    for k in range(count):
        term = dot(g_ref[0, idx_ref[2 + k]], refs[k][...], TN)
        total = term if total is None else total + term
    out_ref[...] = total.astype(out_ref.dtype)


def weight_part(idx, gathered, blocks, width, dtype):
    count = len(blocks)
    kb, feats = blocks[0].shape
    tile = 256
    return pl.pallas_call(
        functools.partial(weight_kernel, count),
        grid_spec=pltpu.PrefetchScalarGridSpec(
            num_scalar_prefetch=1,
            grid=(feats // tile,),
            in_specs=[
                pl.BlockSpec((1, count, kb, width), lambda i, s: (s[0], 0, 0, s[1]))
            ]
            + [pl.BlockSpec((kb, tile), lambda i, s: (0, i))] * count,
            out_specs=pl.BlockSpec((width, tile), lambda i, s: (0, i)),
        ),
        out_shape=jax.ShapeDtypeStruct((width, feats), dtype),
        compiler_params=pltpu.CompilerParams(vmem_limit_bytes=32 * 1024 * 1024),
        cost_estimate=pl.CostEstimate(
            flops=2 * count * kb * feats * width,
            bytes_accessed=2 * count * kb * feats,
            transcendentals=0,
        ),
        name="weight",
    )(idx, gathered, *blocks)


def local(queries, kv_proj, hidden, grad_out, doc_lengths, slab_offsets):
    i32, f32, bf16 = jnp.int32, jnp.float32, jnp.bfloat16
    n = lax.axis_size("ctx")
    dp = lax.axis_size("dp")
    me = lax.axis_index("ctx")
    my_dp = lax.axis_index("dp")
    repeat = n // KV_HEADS
    rows, width = queries.shape[1:]
    kb, kv_width = kv_proj.shape[1:]
    feats = hidden.shape[2] // n
    hw = width // n
    total_rows = rows * n
    keys = kb * n

    bounds = jnp.cumsum(doc_lengths[0], dtype=i32)
    offset = slab_offsets[0]
    index = jnp.arange(total_rows, dtype=i32)
    pos = offset + index
    start = jnp.max(jnp.where(bounds[None, :] <= pos[:, None], bounds[None, :], 0), axis=1)
    low = jnp.maximum(index + 1, jnp.maximum(start, 0) - offset + WINDOW)
    first = low[::BLK] // BLK

    def spread(x, w):
        x = x.reshape(x.shape[0], n, w).transpose(1, 0, 2)
        return lax.all_to_all(x, "ctx", 0, 0, tiled=True).reshape(-1, w)

    copies = jnp.broadcast_to(
        kv_proj[0].reshape(kb, KV_HEADS, 1, 2 * HD).transpose(1, 2, 0, 3),
        (KV_HEADS, repeat, kb, 2 * HD),
    ).reshape(n, kb, 2 * HD)
    kv = lax.all_to_all(copies, "ctx", 0, 0, tiled=True).reshape(keys, 2 * HD)
    q = spread(queries[0], hw)
    go = spread(grad_out[0], hw)

    slices = [
        lax.dynamic_slice_in_dim(hidden[0], (me ^ k) * feats, feats, 1) for k in range(n)
    ]
    q, go, kv, slices = lax.optimization_barrier((q, go, kv, slices))
    blocks = [slices[0]] + [
        lax.ppermute(slices[k], "ctx", [(i, i ^ k) for i in range(n)]) for k in range(1, n)
    ]

    outs, grads = attention(first, low[None], q, go, kv)

    parts = grads.reshape(repeat, keys // repeat, 2 * HD)
    rank = me % repeat
    mine = lax.dynamic_index_in_dim(parts, rank, 0, keepdims=False)
    for k in range(1, repeat):
        sent = lax.dynamic_index_in_dim(parts, rank ^ k, 0, keepdims=False)
        mine = mine + lax.ppermute(sent, "ctx", [(i, i ^ k) for i in range(n)])
    gathered = lax.all_gather(mine.astype(bf16), "ctx", axis=0, tiled=True)
    gathered = gathered.reshape(KV_HEADS, n, kb, 2 * HD)
    grad_low = (
        lax.dynamic_index_in_dim(gathered, me, 1, keepdims=False)
        .transpose(1, 0, 2)
        .reshape(kb, kv_width)
    )

    cols = kv_width // dp
    per = 2 * HD // cols
    order = (me ^ jnp.arange(n, dtype=i32)).astype(i32)

    def part(k, dtype):
        t = (my_dp ^ k).astype(i32)
        idx = jnp.concatenate([jnp.stack([t // per, t % per]), order])
        return weight_part(idx, gathered, blocks, cols, dtype)

    sent = []
    for k in sorted(range(1, dp), key=lambda k: (k != 2, k)):
        sent.append(lax.ppermute(part(k, bf16), "dp", [(i, i ^ k) for i in range(dp)]))
    weight = part(0, f32)

    def back(x):
        x = lax.all_to_all(x.reshape(n, rows, hw), "ctx", 0, 0, tiled=True)
        return x.transpose(1, 0, 2).reshape(1, rows, width)

    attended = back(outs[0])
    grad_query = back(outs[1])
    for s in sent:
        weight = weight + s.astype(f32)
    return (attended, grad_query, grad_low[None], weight.T)


def solution(mesh):
    in_specs = (
        P("dp", "ctx", None),
        P("dp", "ctx", None),
        P("dp", "ctx", None),
        P("dp", "ctx", None),
        P("dp", None),
        P("dp"),
    )
    out_specs = (P("dp", "ctx", None), P("dp", "ctx", None), P("dp", "ctx", None), P("ctx", "dp"))
    return jax.shard_map(local, mesh=mesh, in_specs=in_specs, out_specs=out_specs, check_vma=False)
```

```python
import functools

import jax
import jax.numpy as jnp
from jax import lax
from jax.experimental import pallas as pl
from jax.experimental.pallas import tpu as pltpu
from jax.sharding import PartitionSpec as P

HD = 128
KV_HEADS = 4
WINDOW = 2048
BLK = 256
LOG2E = 1.4426950408889634
FACTOR = HD ** (-0.5)
NT = (((1,), (1,)), ((), ()))
NN = (((1,), (0,)), ((), ()))


def dot(a, b, dims=NN):
    return lax.dot_general(a, b, dims, preferred_element_type=jnp.float32)


def attention_kernel(
    heads, n, low_ref, q_hbm, go_hbm, kv_hbm, hid_hbm,
    att_hbm, gq_hbm, hid_out, grads_ref,
    q_all, go_all, kv_all, att_all, gq_all,
    scores, kt, vt, qs, gs, wlow, dlow, mx, tot, acc, delta,
    send, recv, own, out_send, out_recv, out_own,
):
    f32, bf16 = jnp.float32, jnp.bfloat16
    me = lax.axis_index("ctx")
    rows, kb = q_hbm.shape[0], kv_hbm.shape[0]
    width, feats = heads * HD, hid_out.shape[2]
    repeat = n // KV_HEADS
    chunks = kt.shape[0]
    span = scores.shape[0]
    per = BLK // rows

    def mod(k):
        return lax.rem(me + k, n)

    barrier = pltpu.get_barrier_semaphore()
    for k in range(1, n):
        pl.semaphore_signal(
            barrier, inc=1, device_id={"ctx": mod(k)}, device_id_type=pl.DeviceIdType.MESH
        )
    pl.semaphore_wait(barrier, n - 1)

    def ends(a, dest, source):
        if a == 0:
            cols = pl.ds(pl.multiple_of((dest // repeat) * (2 * HD), 2 * HD), 2 * HD)
            return kv_hbm.at[:, cols], kv_all.at[pl.ds(pl.multiple_of(source * kb, kb), kb)]
        if a == 3:
            cols = pl.ds(pl.multiple_of(dest * feats, feats), feats)
            return hid_hbm.at[:, cols], hid_out.at[source]
        cols = pl.ds(pl.multiple_of(dest * width, width), width)
        where = pl.ds(pl.multiple_of(source * rows, rows), rows)
        src, dst = ((q_hbm, q_all), (go_hbm, go_all))[a - 1]
        return src.at[:, cols], dst.at[where]

    def remote(a, dest, source):
        src, dst = ends(a, dest, source)
        return pltpu.make_async_remote_copy(
            src_ref=src,
            dst_ref=dst,
            send_sem=send.at[a, dest],
            recv_sem=recv.at[a, source],
            device_id={"ctx": dest},
            device_id_type=pl.DeviceIdType.MESH,
        )

    def here(a):
        src, dst = ends(a, me, me)
        return pltpu.make_async_copy(src, dst, own.at[a])

    for a in range(4):
        for k in range(1, n):
            remote(a, mod(k), me).start()
        here(a).start()

    grads_ref[...] = jnp.zeros_like(grads_ref)
    lane = lax.broadcasted_iota(jnp.int32, (BLK, BLK), 1)
    sub = lax.broadcasted_iota(jnp.int32, (BLK, BLK), 0)

    for a in range(3):
        here(a).wait()
        for k in range(1, n):
            remote(a, me, mod(k)).wait_recv()

    def prep(c, carry):
        keys = pl.ds(pl.multiple_of(c * BLK, BLK), BLK)
        kt[c] = kv_all[keys, :HD].astype(f32).T.astype(bf16)
        vt[c] = kv_all[keys, HD:].astype(f32).T.astype(bf16)
        return carry

    lax.fori_loop(0, chunks, prep, 0)

    def out_ends(which, dest, source):
        cols = pl.ds(pl.multiple_of(source * width, width), width)
        where = pl.ds(pl.multiple_of(dest * rows, rows), rows)
        src, dst = ((att_all, att_hbm), (gq_all, gq_hbm))[which]
        return src.at[where], dst.at[:, cols]

    def out_remote(which, dest, source):
        src, dst = out_ends(which, dest, source)
        return pltpu.make_async_remote_copy(
            src_ref=src,
            dst_ref=dst,
            send_sem=out_send.at[which, dest],
            recv_sem=out_recv.at[which, source],
            device_id={"ctx": dest},
            device_id_type=pl.DeviceIdType.MESH,
        )

    def out_here(which):
        src, dst = out_ends(which, me, me)
        return pltpu.make_async_copy(src, dst, out_own.at[which])

    def block(qb, carry):
        mine = pl.ds(pl.multiple_of(qb * BLK, BLK), BLK)
        for h in range(heads):
            qs[h * BLK : (h + 1) * BLK] = q_all[mine, h * HD : (h + 1) * HD]
            gs[h * BLK : (h + 1) * BLK] = go_all[mine, h * HD : (h + 1) * HD]
        mx[...] = jnp.full(mx.shape, -1e30, f32)
        tot[...] = jnp.zeros(tot.shape, f32)
        acc[...] = jnp.zeros(acc.shape, f32)
        low = low_ref[qb]

        def score_step(t, carry):
            c = qb + t
            keys = pl.ds(pl.multiple_of(c * BLK, BLK), BLK)
            key = kv_all[keys, :HD]
            j = sub + c * BLK
            ok = (j >= low) & (j <= lane + (qb * BLK + WINDOW))
            for h in range(heads):
                cols = slice(h * BLK, (h + 1) * BLK)
                s = dot(key, qs[cols, :], NT)
                s = jnp.where(ok, s, -1e30)
                scores[t, :, cols] = s
                part = jnp.max(s.reshape(BLK // 8, 8, BLK), axis=0)
                mx[:, cols] = jnp.maximum(mx[:, cols], part)
            return carry

        lax.fori_loop(0, span, score_step, 0)
        mx[0:1, :] = jnp.max(mx[...], axis=0, keepdims=True) * (FACTOR * LOG2E)

        def value_step(t, carry):
            for h in range(heads):
                cols = slice(h * BLK, (h + 1) * BLK)
                p = jnp.exp2(scores[t, :, cols] * (FACTOR * LOG2E) - mx[0:1, cols])
                scores[t, :, cols] = p
                tot[:, cols] += jnp.sum(p.reshape(BLK // 8, 8, BLK), axis=0)
                acc[:, cols] += dot(vt[qb + t], p.astype(bf16))
            return carry

        lax.fori_loop(0, span, value_step, 0)
        tot[0:1, :] = 1.0 / jnp.sum(tot[...], axis=0, keepdims=True)
        for h in range(heads):
            cols = slice(h * BLK, (h + 1) * BLK)
            att = (acc[:, cols] * tot[0:1, cols]).T.astype(bf16)
            att_all[mine, h * HD : (h + 1) * HD] = att
            prod = att.astype(f32) * gs[cols, :].astype(f32)
            delta[0:1, cols] = jnp.sum(prod.T, axis=0, keepdims=True)
        acc[...] = jnp.zeros(acc.shape, f32)

        def grad_step(t, carry):
            keys = pl.ds(pl.multiple_of((qb + t) * BLK, BLK), BLK)
            value = kv_all[keys, HD:]
            for h in range(heads):
                cols = slice(h * BLK, (h + 1) * BLK)
                w = scores[t, :, cols] * tot[0:1, cols]
                gp = dot(value, gs[cols, :], NT)
                ds = (w * (gp - delta[0:1, cols])).astype(bf16)
                wlow[:, cols] = w.astype(bf16)
                dlow[:, cols] = ds
                acc[:, cols] += dot(kt[qb + t], ds)
            grads_ref[keys, :HD] += dot(dlow[...], qs[...]) * FACTOR
            grads_ref[keys, HD:] += dot(wlow[...], gs[...])
            return carry

        lax.fori_loop(0, span, grad_step, 0)
        for h in range(heads):
            cols = slice(h * BLK, (h + 1) * BLK)
            gq_all[mine, h * HD : (h + 1) * HD] = (acc[:, cols] * FACTOR).T.astype(bf16)
        for u in range(per):
            dest = qb * per + u

            @pl.when(dest == me)
            def _():
                for which in range(2):
                    out_here(which).start()

            @pl.when(dest != me)
            def _():
                for which in range(2):
                    out_remote(which, dest, me).start()

        return carry

    lax.fori_loop(0, q_all.shape[0] // BLK, block, 0)

    here(3).wait()
    for which in range(2):
        out_here(which).wait()
    for k in range(1, n):
        remote(3, me, mod(k)).wait_recv()
        for which in range(2):
            out_remote(which, me, mod(k)).wait_recv()
    for k in range(1, n):
        for a in range(4):
            remote(a, mod(k), me).wait_send()
        for which in range(2):
            out_remote(which, mod(k), me).wait_send()


def attention(low, queries, grad_out, kv_proj, hidden):
    n = lax.axis_size("ctx")
    rows, total_width = queries.shape
    kb = kv_proj.shape[0]
    width, feats = total_width // n, hidden.shape[1] // n
    total, keys = rows * n, kb * n
    heads = width // HD
    f32, bf16 = jnp.float32, jnp.bfloat16
    wide = heads * BLK
    span = WINDOW // BLK + 1
    chunks = keys // BLK
    hbm = pl.BlockSpec(memory_space=pl.ANY)
    vmem = pl.BlockSpec(memory_space=pltpu.VMEM)
    dma = pltpu.SemaphoreType.DMA
    return pl.pallas_call(
        functools.partial(attention_kernel, heads, n),
        in_specs=[vmem, hbm, hbm, hbm, hbm],
        out_specs=[hbm, hbm, hbm, vmem],
        scratch_shapes=[
            pltpu.VMEM((total, width), bf16),
            pltpu.VMEM((total, width), bf16),
            pltpu.VMEM((keys, 2 * HD), bf16),
            pltpu.VMEM((total, width), bf16),
            pltpu.VMEM((total, width), bf16),
            pltpu.VMEM((span, BLK, wide), f32),
            pltpu.VMEM((chunks, HD, BLK), bf16),
            pltpu.VMEM((chunks, HD, BLK), bf16),
            pltpu.VMEM((wide, HD), bf16),
            pltpu.VMEM((wide, HD), bf16),
            pltpu.VMEM((BLK, wide), bf16),
            pltpu.VMEM((BLK, wide), bf16),
            pltpu.VMEM((8, wide), f32),
            pltpu.VMEM((8, wide), f32),
            pltpu.VMEM((HD, wide), f32),
            pltpu.VMEM((8, wide), f32),
            dma((4, n)),
            dma((4, n)),
            dma((4,)),
            dma((2, n)),
            dma((2, n)),
            dma((2,)),
        ],
        out_shape=[
            jax.ShapeDtypeStruct((rows, total_width), bf16),
            jax.ShapeDtypeStruct((rows, total_width), bf16),
            jax.ShapeDtypeStruct((n, kb, feats), bf16),
            jax.ShapeDtypeStruct((keys, 2 * HD), f32),
        ],
        compiler_params=pltpu.CompilerParams(
            collective_id=0, has_side_effects=True, vmem_limit_bytes=52 * 1024 * 1024
        ),
        cost_estimate=pl.CostEstimate(
            flops=20 * total * (WINDOW + BLK) * width,
            bytes_accessed=12 * total * width,
            transcendentals=total * (WINDOW + BLK) * heads,
        ),
        name="attention",
    )(low, queries, grad_out, kv_proj, hidden)


def weight_kernel(idx_ref, g_ref, hid_ref, out_ref):
    total = dot(g_ref[0, 0], hid_ref[0])
    for r in range(1, hid_ref.shape[0]):
        total = total + dot(g_ref[0, r], hid_ref[r])
    out_ref[...] = total.astype(out_ref.dtype)


def weight_part(idx, gathered, hidden, width, dtype):
    repeat, kr, feats = hidden.shape
    tile = 256 if feats % 512 else 512
    return pl.pallas_call(
        weight_kernel,
        grid_spec=pltpu.PrefetchScalarGridSpec(
            num_scalar_prefetch=1,
            grid=(pl.cdiv(feats, tile),),
            in_specs=[
                pl.BlockSpec((1, repeat, width, kr), lambda i, s: (s[0], 0, s[1], 0)),
                pl.BlockSpec((repeat, kr, tile), lambda i, s: (0, 0, i)),
            ],
            out_specs=pl.BlockSpec((width, tile), lambda i, s: (0, i)),
        ),
        out_shape=jax.ShapeDtypeStruct((width, feats), dtype),
        compiler_params=pltpu.CompilerParams(vmem_limit_bytes=32 * 1024 * 1024),
        cost_estimate=pl.CostEstimate(
            flops=2 * repeat * kr * feats * width,
            bytes_accessed=2 * repeat * kr * feats,
            transcendentals=0,
        ),
        name="weight",
    )(idx, gathered, hidden)


def local(queries, kv_proj, hidden, grad_out, doc_lengths, slab_offsets):
    i32, f32, bf16 = jnp.int32, jnp.float32, jnp.bfloat16
    n = lax.axis_size("ctx")
    dp = lax.axis_size("dp")
    me = lax.axis_index("ctx")
    my_dp = lax.axis_index("dp")
    repeat = n // KV_HEADS
    rows = queries.shape[1]
    kb, kv_width = kv_proj.shape[1:]
    total_rows = rows * n
    keys = kb * n

    bounds = jnp.cumsum(doc_lengths[0], dtype=i32)
    offset = slab_offsets[0]
    index = jnp.arange(total_rows, dtype=i32)
    pos = offset + index
    start = jnp.max(jnp.where(bounds[None, :] <= pos[:, None], bounds[None, :], 0), axis=1)
    low = jnp.maximum(index + 1, jnp.maximum(start, 0) - offset + WINDOW)
    low = low.reshape(total_rows // BLK, 1, BLK)
    attended, grad_query, hid, grads = attention(
        low, queries[0], grad_out[0], kv_proj[0], hidden[0]
    )
    kr = keys // repeat
    hid = hid.reshape(repeat, kr, hid.shape[2])

    parts = grads.reshape(repeat, keys // repeat, 2 * HD)
    rank = me % repeat
    mine = lax.dynamic_index_in_dim(parts, rank, 0, keepdims=False)
    for k in range(1, repeat):
        sent = lax.dynamic_index_in_dim(parts, rank ^ k, 0, keepdims=False)
        mine = mine + lax.ppermute(sent, "ctx", [(i, i ^ k) for i in range(n)])
    gathered = lax.all_gather(mine.astype(bf16).T, "ctx", axis=0)
    gathered = gathered.reshape(KV_HEADS, repeat, 2 * HD, kr)
    mine_low = lax.dynamic_index_in_dim(gathered, me * kb // kr, 1, keepdims=False)
    mine_low = lax.dynamic_slice_in_dim(mine_low, me * kb % kr, kb, 2)
    grad_low = mine_low.transpose(2, 0, 1).reshape(kb, kv_width)

    cols = kv_width // dp
    per = 2 * HD // cols

    def part(k, dtype):
        t = (my_dp ^ k).astype(i32)
        return weight_part(jnp.stack([t // per, t % per]), gathered, hid, cols, dtype)

    sent = []
    for k in sorted(range(1, dp), key=lambda k: (k != 2, k)):
        sent.append(lax.ppermute(part(k, bf16), "dp", [(i, i ^ k) for i in range(dp)]))
    weight = part(0, f32)

    for s in sent:
        weight = weight + s.astype(f32)
    return (attended[None], grad_query[None], grad_low[None], weight.T)


def solution(mesh):
    in_specs = (
        P("dp", "ctx", None),
        P("dp", "ctx", None),
        P("dp", "ctx", None),
        P("dp", "ctx", None),
        P("dp", None),
        P("dp"),
    )
    out_specs = (P("dp", "ctx", None), P("dp", "ctx", None), P("dp", "ctx", None), P("ctx", "dp"))
    return jax.shard_map(local, mesh=mesh, in_specs=in_specs, out_specs=out_specs, check_vma=False)
```

```python
import functools

import jax
import jax.numpy as jnp
from jax import lax
from jax.experimental import pallas as pl
from jax.experimental.pallas import tpu as pltpu
from jax.sharding import PartitionSpec as P

HD = 128
KV_HEADS = 4
WINDOW = 2048
BLK = 256
LOG2E = 1.4426950408889634
FACTOR = HD ** (-0.5)
NT = (((1,), (1,)), ((), ()))
NN = (((1,), (0,)), ((), ()))


def dot(a, b, dims=NN):
    return lax.dot_general(a, b, dims, preferred_element_type=jnp.float32)


def attention_kernel(
    heads, n, low_ref, q_hbm, go_hbm, kv_hbm, hid_hbm,
    att_hbm, gq_hbm, hid_out, grads_ref,
    q_all, go_all, kv_all, att_all, gq_all,
    scores, kt, vt, qs, gs, wlow, dlow, mx, tot, acc, delta,
    send, recv, own, out_send, out_recv, out_own,
):
    f32, bf16 = jnp.float32, jnp.bfloat16
    me = lax.axis_index("ctx")
    rows, kb = q_hbm.shape[0], kv_hbm.shape[0]
    width, feats = heads * HD, hid_out.shape[2]
    repeat = n // KV_HEADS
    chunks = kt.shape[0]
    span = scores.shape[0]
    per = BLK // rows

    def mod(k):
        return lax.rem(me + k, n)

    barrier = pltpu.get_barrier_semaphore()
    for k in range(1, n):
        pl.semaphore_signal(
            barrier, inc=1, device_id={"ctx": mod(k)}, device_id_type=pl.DeviceIdType.MESH
        )
    pl.semaphore_wait(barrier, n - 1)

    def ends(a, dest, source):
        if a == 0:
            cols = pl.ds(pl.multiple_of((dest // repeat) * (2 * HD), 2 * HD), 2 * HD)
            return kv_hbm.at[:, cols], kv_all.at[pl.ds(pl.multiple_of(source * kb, kb), kb)]
        if a == 3:
            cols = pl.ds(pl.multiple_of(dest * feats, feats), feats)
            return hid_hbm.at[:, cols], hid_out.at[source]
        cols = pl.ds(pl.multiple_of(dest * width, width), width)
        where = pl.ds(pl.multiple_of(source * rows, rows), rows)
        src, dst = ((q_hbm, q_all), (go_hbm, go_all))[a - 1]
        return src.at[:, cols], dst.at[where]

    def remote(a, dest, source):
        src, dst = ends(a, dest, source)
        return pltpu.make_async_remote_copy(
            src_ref=src,
            dst_ref=dst,
            send_sem=send.at[a, dest],
            recv_sem=recv.at[a, source],
            device_id={"ctx": dest},
            device_id_type=pl.DeviceIdType.MESH,
        )

    def here(a):
        src, dst = ends(a, me, me)
        return pltpu.make_async_copy(src, dst, own.at[a])

    def begin(a):
        for k in range(1, n):
            remote(a, mod(k), me).start()
        here(a).start()

    for a in range(3):
        begin(a)

    grads_ref[...] = jnp.zeros_like(grads_ref)
    lane = lax.broadcasted_iota(jnp.int32, (BLK, BLK), 1)
    sub = lax.broadcasted_iota(jnp.int32, (BLK, BLK), 0)

    for a in range(3):
        here(a).wait()
        for k in range(1, n):
            remote(a, me, mod(k)).wait_recv()
    begin(3)

    def prep(c, carry):
        keys = pl.ds(pl.multiple_of(c * BLK, BLK), BLK)
        kt[c] = kv_all[keys, :HD].astype(f32).T.astype(bf16)
        vt[c] = kv_all[keys, HD:].astype(f32).T.astype(bf16)
        return carry

    lax.fori_loop(0, chunks, prep, 0)

    def out_ends(which, dest, source):
        cols = pl.ds(pl.multiple_of(source * width, width), width)
        where = pl.ds(pl.multiple_of(dest * rows, rows), rows)
        src, dst = ((att_all, att_hbm), (gq_all, gq_hbm))[which]
        return src.at[where], dst.at[:, cols]

    def out_remote(which, dest, source):
        src, dst = out_ends(which, dest, source)
        return pltpu.make_async_remote_copy(
            src_ref=src,
            dst_ref=dst,
            send_sem=out_send.at[which, dest],
            recv_sem=out_recv.at[which, source],
            device_id={"ctx": dest},
            device_id_type=pl.DeviceIdType.MESH,
        )

    def out_here(which):
        src, dst = out_ends(which, me, me)
        return pltpu.make_async_copy(src, dst, out_own.at[which])

    def block(qb, carry):
        mine = pl.ds(pl.multiple_of(qb * BLK, BLK), BLK)
        for h in range(heads):
            qs[h * BLK : (h + 1) * BLK] = q_all[mine, h * HD : (h + 1) * HD]
            gs[h * BLK : (h + 1) * BLK] = go_all[mine, h * HD : (h + 1) * HD]
        mx[...] = jnp.full(mx.shape, -1e30, f32)
        tot[...] = jnp.zeros(tot.shape, f32)
        acc[...] = jnp.zeros(acc.shape, f32)
        low = low_ref[qb]

        def score_step(t, carry):
            c = qb + t
            keys = pl.ds(pl.multiple_of(c * BLK, BLK), BLK)
            key = kv_all[keys, :HD]
            j = sub + c * BLK
            ok = (j >= low) & (j <= lane + (qb * BLK + WINDOW))
            for h in range(heads):
                cols = slice(h * BLK, (h + 1) * BLK)
                s = dot(key, qs[cols, :], NT)
                s = jnp.where(ok, s, -1e30)
                scores[t, :, cols] = s
                part = jnp.max(s.reshape(BLK // 8, 8, BLK), axis=0)
                mx[:, cols] = jnp.maximum(mx[:, cols], part)
            return carry

        lax.fori_loop(0, span, score_step, 0)
        mx[0:1, :] = jnp.max(mx[...], axis=0, keepdims=True) * (FACTOR * LOG2E)

        def value_step(t, carry):
            for h in range(heads):
                cols = slice(h * BLK, (h + 1) * BLK)
                p = jnp.exp2(scores[t, :, cols] * (FACTOR * LOG2E) - mx[0:1, cols])
                scores[t, :, cols] = p
                tot[:, cols] += jnp.sum(p.reshape(BLK // 8, 8, BLK), axis=0)
                acc[:, cols] += dot(vt[qb + t], p.astype(bf16))
            return carry

        lax.fori_loop(0, span, value_step, 0)
        tot[0:1, :] = 1.0 / jnp.sum(tot[...], axis=0, keepdims=True)
        for h in range(heads):
            cols = slice(h * BLK, (h + 1) * BLK)
            att = (acc[:, cols] * tot[0:1, cols]).T.astype(bf16)
            att_all[mine, h * HD : (h + 1) * HD] = att
            prod = att.astype(f32) * gs[cols, :].astype(f32)
            delta[0:1, cols] = jnp.sum(prod.T, axis=0, keepdims=True)
        acc[...] = jnp.zeros(acc.shape, f32)

        def grad_step(t, carry):
            keys = pl.ds(pl.multiple_of((qb + t) * BLK, BLK), BLK)
            value = kv_all[keys, HD:]
            for h in range(heads):
                cols = slice(h * BLK, (h + 1) * BLK)
                w = scores[t, :, cols] * tot[0:1, cols]
                gp = dot(value, gs[cols, :], NT)
                ds = (w * (gp - delta[0:1, cols])).astype(bf16)
                wlow[:, cols] = w.astype(bf16)
                dlow[:, cols] = ds
                acc[:, cols] += dot(kt[qb + t], ds)
            grads_ref[keys, :HD] += dot(dlow[...], qs[...]) * FACTOR
            grads_ref[keys, HD:] += dot(wlow[...], gs[...])
            return carry

        lax.fori_loop(0, span, grad_step, 0)
        for h in range(heads):
            cols = slice(h * BLK, (h + 1) * BLK)
            gq_all[mine, h * HD : (h + 1) * HD] = (acc[:, cols] * FACTOR).T.astype(bf16)
        for u in range(per):
            dest = qb * per + u

            @pl.when(dest == me)
            def _():
                for which in range(2):
                    out_here(which).start()

            @pl.when(dest != me)
            def _():
                for which in range(2):
                    out_remote(which, dest, me).start()

        return carry

    lax.fori_loop(0, q_all.shape[0] // BLK, block, 0)

    here(3).wait()
    for which in range(2):
        out_here(which).wait()
    for k in range(1, n):
        remote(3, me, mod(k)).wait_recv()
        for which in range(2):
            out_remote(which, me, mod(k)).wait_recv()
    for k in range(1, n):
        for a in range(4):
            remote(a, mod(k), me).wait_send()
        for which in range(2):
            out_remote(which, mod(k), me).wait_send()


def attention(low, queries, grad_out, kv_proj, hidden):
    n = lax.axis_size("ctx")
    rows, total_width = queries.shape
    kb = kv_proj.shape[0]
    width, feats = total_width // n, hidden.shape[1] // n
    total, keys = rows * n, kb * n
    heads = width // HD
    f32, bf16 = jnp.float32, jnp.bfloat16
    wide = heads * BLK
    span = WINDOW // BLK + 1
    chunks = keys // BLK
    hbm = pl.BlockSpec(memory_space=pl.ANY)
    vmem = pl.BlockSpec(memory_space=pltpu.VMEM)
    dma = pltpu.SemaphoreType.DMA
    return pl.pallas_call(
        functools.partial(attention_kernel, heads, n),
        in_specs=[vmem, hbm, hbm, hbm, hbm],
        out_specs=[hbm, hbm, hbm, vmem],
        scratch_shapes=[
            pltpu.VMEM((total, width), bf16),
            pltpu.VMEM((total, width), bf16),
            pltpu.VMEM((keys, 2 * HD), bf16),
            pltpu.VMEM((total, width), bf16),
            pltpu.VMEM((total, width), bf16),
            pltpu.VMEM((span, BLK, wide), f32),
            pltpu.VMEM((chunks, HD, BLK), bf16),
            pltpu.VMEM((chunks, HD, BLK), bf16),
            pltpu.VMEM((wide, HD), bf16),
            pltpu.VMEM((wide, HD), bf16),
            pltpu.VMEM((BLK, wide), bf16),
            pltpu.VMEM((BLK, wide), bf16),
            pltpu.VMEM((8, wide), f32),
            pltpu.VMEM((8, wide), f32),
            pltpu.VMEM((HD, wide), f32),
            pltpu.VMEM((8, wide), f32),
            dma((4, n)),
            dma((4, n)),
            dma((4,)),
            dma((2, n)),
            dma((2, n)),
            dma((2,)),
        ],
        out_shape=[
            jax.ShapeDtypeStruct((rows, total_width), bf16),
            jax.ShapeDtypeStruct((rows, total_width), bf16),
            jax.ShapeDtypeStruct((n, kb, feats), bf16),
            jax.ShapeDtypeStruct((keys, 2 * HD), f32),
        ],
        compiler_params=pltpu.CompilerParams(
            collective_id=0, has_side_effects=True, vmem_limit_bytes=52 * 1024 * 1024
        ),
        cost_estimate=pl.CostEstimate(
            flops=20 * total * (WINDOW + BLK) * width,
            bytes_accessed=12 * total * width,
            transcendentals=total * (WINDOW + BLK) * heads,
        ),
        name="attention",
    )(low, queries, grad_out, kv_proj, hidden)


def weight_kernel(idx_ref, g_ref, hid_ref, out_ref):
    total = dot(g_ref[0, 0], hid_ref[0])
    for r in range(1, hid_ref.shape[0]):
        total = total + dot(g_ref[0, r], hid_ref[r])
    out_ref[...] = total.astype(out_ref.dtype)


def weight_part(idx, gathered, hidden, width, dtype):
    repeat, kr, feats = hidden.shape
    tile = 256 if feats % 512 else 512
    return pl.pallas_call(
        weight_kernel,
        grid_spec=pltpu.PrefetchScalarGridSpec(
            num_scalar_prefetch=1,
            grid=(pl.cdiv(feats, tile),),
            in_specs=[
                pl.BlockSpec((1, repeat, width, kr), lambda i, s: (s[0], 0, s[1], 0)),
                pl.BlockSpec((repeat, kr, tile), lambda i, s: (0, 0, i)),
            ],
            out_specs=pl.BlockSpec((width, tile), lambda i, s: (0, i)),
        ),
        out_shape=jax.ShapeDtypeStruct((width, feats), dtype),
        compiler_params=pltpu.CompilerParams(vmem_limit_bytes=32 * 1024 * 1024),
        cost_estimate=pl.CostEstimate(
            flops=2 * repeat * kr * feats * width,
            bytes_accessed=2 * repeat * kr * feats,
            transcendentals=0,
        ),
        name="weight",
    )(idx, gathered, hidden)


def local(queries, kv_proj, hidden, grad_out, doc_lengths, slab_offsets):
    i32, f32, bf16 = jnp.int32, jnp.float32, jnp.bfloat16
    n = lax.axis_size("ctx")
    dp = lax.axis_size("dp")
    me = lax.axis_index("ctx")
    my_dp = lax.axis_index("dp")
    repeat = n // KV_HEADS
    rows = queries.shape[1]
    kb, kv_width = kv_proj.shape[1:]
    total_rows = rows * n
    keys = kb * n

    bounds = jnp.cumsum(doc_lengths[0], dtype=i32)
    offset = slab_offsets[0]
    index = jnp.arange(total_rows, dtype=i32)
    pos = offset + index
    start = jnp.max(jnp.where(bounds[None, :] <= pos[:, None], bounds[None, :], 0), axis=1)
    low = jnp.maximum(index + 1, jnp.maximum(start, 0) - offset + WINDOW)
    low = low.reshape(total_rows // BLK, 1, BLK)
    attended, grad_query, hid, grads = attention(
        low, queries[0], grad_out[0], kv_proj[0], hidden[0]
    )
    kr = keys // repeat
    hid = hid.reshape(repeat, kr, hid.shape[2])

    parts = grads.reshape(repeat, keys // repeat, 2 * HD)
    rank = me % repeat
    mine = lax.dynamic_index_in_dim(parts, rank, 0, keepdims=False)
    for k in range(1, repeat):
        sent = lax.dynamic_index_in_dim(parts, rank ^ k, 0, keepdims=False)
        mine = mine + lax.ppermute(sent, "ctx", [(i, i ^ k) for i in range(n)])
    cols = kv_width // dp
    per = 2 * HD // cols
    half = cols // 2
    pieces = mine.astype(bf16).T.reshape(per, 2, half, kr)
    gathers = [
        lax.all_gather(pieces[:, p].reshape(per * half, kr), "ctx", axis=0).reshape(
            KV_HEADS, repeat, per * half, kr
        )
        for p in range(2)
    ]

    def own_rows(gathered):
        x = lax.dynamic_index_in_dim(gathered, me * kb // kr, 1, keepdims=False)
        x = lax.dynamic_slice_in_dim(x, me * kb % kr, kb, 2)
        return x.reshape(KV_HEADS, per, half, kb)

    grad_low = jnp.stack([own_rows(g) for g in gathers], axis=2).reshape(kv_width, kb).T

    def part(k, p, dtype):
        t = (my_dp ^ k).astype(i32)
        return weight_part(jnp.stack([t // per, t % per]), gathers[p], hid, half, dtype)

    order = sorted(range(1, dp), key=lambda k: (k != 2, k))
    sums = []
    for p in range(2):
        sent = [
            lax.ppermute(part(k, p, bf16), "dp", [(i, i ^ k) for i in range(dp)]) for k in order
        ]
        weight = part(0, p, f32)
        for other in sent:
            weight = weight + other.astype(f32)
        sums.append(weight)
    weight = jnp.concatenate(sums, axis=0)
    return (attended[None], grad_query[None], grad_low[None], weight.T)


def solution(mesh):
    in_specs = (
        P("dp", "ctx", None),
        P("dp", "ctx", None),
        P("dp", "ctx", None),
        P("dp", "ctx", None),
        P("dp", None),
        P("dp"),
    )
    out_specs = (P("dp", "ctx", None), P("dp", "ctx", None), P("dp", "ctx", None), P("ctx", "dp"))
    return jax.shard_map(local, mesh=mesh, in_specs=in_specs, out_specs=out_specs, check_vma=False)
```
